256 devices in a mesh: mod: 16 (over z, y_hi), mode: 16 (over y_lo, x, core).
Axes of the slice: x: 4, y: 4 (y_hi: 2, y_lo: 2; y = y_hi * 2 + y_lo), z: 8, core: 2. Of those that a mesh axis runs over, the one named last changes fastest.
Arguments:
- mod_points: int32 [16], P('mod'), may hold values from 0 to 47
- pupil_mask: int32 [256, 256], P('mode'), may hold values 0 or 1
- phase_offset: float32 [256, 256], P('mode'), may hold values from -6 to 6
- modes: bfloat16 [64, 256, 256], P('mode', 'mod'), may hold values from -6 to 6
- block_map: int32 [16], replicated, may hold values from 0 to 15, each once
Outputs:
- tangent: float32 [512, 64, 512], P('mod', 'mode')
The draws below stay inside these ranges and needn't reach their ends.
Inputs may be any that keep to these rules, and one draw needn't show every extreme that they name: `mod_points`: indices of points on a circle of 48 equally spaced modulation points; repeats are allowed. `block_map`: each of the 16 detector row blocks appears exactly once.
All inputs are finite; a program needn't handle non-finite values. No bound on the sum of `pupil_mask` on one device may be relied on, other than what follows from the above.
Results may differ from the reference program's by a relative error of at most 0.015.
Values may be sent and summed in bfloat16 or wider, within the bound.
No kernel may reach another device: no remote copies, remote signals or barrier semaphores. Data moves between devices by JAX's collectives and lax.ppermute only.
A program may use at most 64 MiB of HBM per device.

```python
import math
import jax
import jax.numpy as jnp
from jax import lax

PUPIL = 256
PADDED = 512
NMODES = 64
MODS = 16
NPTS = 48
NBLK = 16


def place_ends(values, stream_key, least, high):
    place = [jax.random.randint(jax.random.fold_in(stream_key, axis), (), 0, length) for axis, length in enumerate(values.shape)]
    longest = values.shape.index(max(values.shape))
    neighbour = place[:longest] + [(place[longest] + 1) % values.shape[longest]] + place[longest + 1:]
    return values.at[tuple(place)].set(least).at[tuple(neighbour)].set(high)


def shard_levels(stream_key, dims, cuts, smallest, largest):
    gain = 1.0
    for dim, blocks in cuts:
        heights = jax.random.uniform(jax.random.fold_in(jax.random.fold_in(stream_key, 6), dim), (blocks,), jnp.float32, smallest / len(cuts), largest / len(cuts))
        gain = gain * jnp.repeat(jnp.exp(heights), dims[dim] // blocks).reshape((-1,) + (1,) * (len(dims) - 1 - dim))
    return gain


def normal_values(own_key, shape, spread, reach, pieces=(), kind=jnp.bfloat16):
    result = spread * jax.random.normal(own_key, shape, jnp.float32)
    if pieces:
        result = result * shard_levels(own_key, shape, pieces, -0.22, 0.18)
    return jnp.clip(result, -reach, reach).astype(kind)


def setup_inputs(seed: int = 0) -> dict:
    streams_of = jax.random.split(jax.random.key(seed), 6)
    return {
        "mod_points": place_ends(jax.random.randint(streams_of[0], (MODS,), 0, NPTS), jax.random.fold_in(streams_of[0], 1), 0, NPTS - 1).astype(jnp.int32),
        "pupil_mask": place_ends((jax.random.randint(streams_of[1], (PUPIL, PUPIL), 0, 8) < 7).astype(jnp.int32), jax.random.fold_in(streams_of[1], 1), 0, 1),
        "phase_offset": normal_values(streams_of[2], (PUPIL, PUPIL), 1.0, 6.0, ((0, 16),), jnp.float32),
        "modes": normal_values(streams_of[3], (NMODES, PUPIL, PUPIL), 1.0, 6.0, ((0, 16), (1, 16))),
        "block_map": jax.random.permutation(streams_of[4], NBLK).astype(jnp.int32),
    }


radius_cells = 6.0

def dft_table(left, right, length):
    turns = left[:, None] * right[None, :] % length
    angle = turns.astype(jnp.float32) * (2.0 * math.pi / length)
    norm = 1.0 / math.sqrt(length)
    return ((jnp.cos(angle) * norm).astype(jnp.bfloat16), (-jnp.sin(angle) * norm).astype(jnp.bfloat16))

def complex_product(form, left, right):
    left_re = left[0].astype(jnp.float32)
    left_im = left[1].astype(jnp.float32)
    right_re = right[0].astype(jnp.float32)
    right_im = right[1].astype(jnp.float32)
    high = lax.Precision.HIGHEST
    real = jnp.einsum(form, left_re, right_re, precision=high) - jnp.einsum(form, left_im, right_im, precision=high)
    imag = jnp.einsum(form, left_re, right_im, precision=high) + jnp.einsum(form, left_im, right_re, precision=high)
    return (real, imag)

def pyramid_parts(length):
    centred = jnp.arange(length, dtype=jnp.int32) - length // 2
    quarter = (jnp.abs(centred)[:, None] + jnp.abs(centred)[None, :]) % 4
    cos_part = (quarter == 0).astype(jnp.float32) - (quarter == 2).astype(jnp.float32)
    sin_part = (quarter == 1).astype(jnp.float32) - (quarter == 3).astype(jnp.float32)
    return (cos_part, sin_part)

def pupil_field(point, phase, mask):
    pupil = phase.shape[0]
    length = 2 * pupil
    theta = point.astype(jnp.float32) * (2.0 * math.pi / NPTS)
    centred = (jnp.arange(pupil, dtype=jnp.int32) - pupil // 2).astype(jnp.float32)
    tilt = 2.0 * math.pi * radius_cells / length * (jnp.cos(theta) * centred[:, None] + jnp.sin(theta) * centred[None, :])
    total = phase + tilt
    return ((mask * jnp.cos(total)).astype(jnp.bfloat16), (mask * jnp.sin(total)).astype(jnp.bfloat16))

def reference(mod_points, pupil_mask, phase_offset, modes, block_map):
    mask = pupil_mask.astype(jnp.float32)
    centred_pad = jnp.arange(PADDED, dtype=jnp.int32) - PADDED // 2
    centred_pupil = jnp.arange(PUPIL, dtype=jnp.int32) - PUPIL // 2
    first = dft_table(centred_pad, centred_pupil, PADDED)
    second = dft_table(centred_pad, centred_pad, PADDED)
    cos_part, sin_part = pyramid_parts(PADDED)
    values = modes.astype(jnp.float32)

    def one_point(total, point):
        field_re, field_im = pupil_field(point, phase_offset, mask)
        moved_re = (-values * field_im.astype(jnp.float32)).astype(jnp.bfloat16)
        moved_im = (values * field_re.astype(jnp.float32)).astype(jnp.bfloat16)
        all_re = jnp.concatenate([field_re[None], moved_re], axis=0)
        all_im = jnp.concatenate([field_im[None], moved_im], axis=0)
        a_re, a_im = complex_product('un,fnp->fup', first, (all_re, all_im))
        a_re = a_re.astype(jnp.bfloat16)
        a_im = a_im.astype(jnp.bfloat16)
        f_re, f_im = complex_product('fup,vp->fuv', (a_re, a_im), first)
        g_re = (cos_part * f_re - sin_part * f_im).astype(jnp.bfloat16)
        g_im = (cos_part * f_im + sin_part * f_re).astype(jnp.bfloat16)
        b_re, b_im = complex_product('um,fmv->fuv', second, (g_re, g_im))
        b_re = b_re.astype(jnp.bfloat16)
        b_im = b_im.astype(jnp.bfloat16)
        d_re, d_im = complex_product('fuv,pv->ufp', (b_re, b_im), second)
        term = 2.0 * (d_re[:, :1] * d_re[:, 1:] + d_im[:, :1] * d_im[:, 1:])
        return (total + term, None)
    start = jnp.zeros((PADDED, NMODES, PADDED), jnp.float32)
    summed = lax.scan(one_point, start, mod_points)[0]
    block_rows = PADDED // NBLK
    ordered = summed.reshape(NBLK, block_rows, NMODES, PADDED)[block_map].reshape(PADDED, NMODES, PADDED)
    return ordered * (float(PADDED * PADDED) / float(PUPIL * PUPIL * MODS))
```

```python
import math

import jax
import jax.numpy as jnp
import numpy as np
from jax import lax
from jax.experimental import pallas as pl
from jax.experimental.pallas import tpu as pltpu
from jax.sharding import PartitionSpec as P

NPTS = 48
radius_cells = 6.0
ORDER = (1, 8, 2, 4)


def sensor_table(length, pupil):
    c = np.arange(length) - length // 2
    n = np.arange(pupil) - pupil // 2
    s = c[:, None] + n[None, :]
    odd = s % 2 != 0
    with np.errstate(divide="ignore"):
        kernel = 2.0 / (length * np.cos(2.0 * np.pi * s / length))
    shift = np.abs(s % length - length // 2) == length // 4
    direct = np.where(shift, np.where(n % 2 == 0, 0.5, -0.5)[None, :], 0.0)
    return np.where(odd, kernel, direct)


def tangent_kernel(block_map, ids, modes_ref, field_ref, rows_ref, second_ref, out_ref, left, base, right, mid, own):
    del block_map
    blocks, height, lanes = modes_ref.shape
    rows, pupil = rows_ref.shape
    fields = out_ref.shape[1]
    me = ids[1]
    for place in range(blocks):
        other = sum(bit for t, bit in enumerate(ORDER) if place >> t & 1)
        block = me ^ other
        part = field_ref[place]
        at = pl.multiple_of(block * 16, 16)
        base[pl.ds(at, 16), :pupil] = part[0]
        base[pl.ds(at, 16), pupil:] = part[1]
    last = height - 16
    point = modes_ref[:, last:, :].astype(jnp.float32)[:, 0, :]
    theta = point * (2.0 * math.pi / NPTS)
    scale = 2.0 * math.pi * radius_cells / (2 * pupil)
    column = lax.broadcasted_iota(jnp.int32, (blocks, pupil), 1)
    odd = column % 2 == 1
    centred = (column - pupil // 2).astype(jnp.float32) * scale

    def factor(tilt):
        angle = jnp.concatenate([tilt] * (pupil // lanes), axis=1) * centred
        cos, sin = jnp.cos(angle), jnp.sin(angle)
        return jnp.where(odd, -sin, cos), jnp.where(odd, cos, sin)

    row_re, row_im = factor(jnp.cos(theta))
    col_re, col_im = factor(jnp.sin(theta))
    table = rows_ref[...]
    for k in range(blocks):
        at = slice(k * rows, (k + 1) * rows)
        left[at, :pupil] = (table * row_re[k : k + 1]).astype(left.dtype)
        left[at, pupil:] = (table * row_im[k : k + 1]).astype(left.dtype)
    half = blocks * rows
    for j in range(fields + 1):
        re = base[:, :pupil]
        im = base[:, pupil:]
        if j == 0:
            right[:pupil, :pupil] = re
            right[:pupil, pupil:] = im
            right[pupil:, :pupil] = -im
            right[pupil:, pupil:] = re
        else:
            at = (j - 1) * 32
            value = jnp.concatenate(
                [modes_ref[:, at : at + 16, :].reshape(pupil, lanes), modes_ref[:, at + 16 : at + 32, :].reshape(pupil, lanes)], axis=1
            )
            real = -value * im
            imag = value * re
            right[:pupil, :pupil] = real
            right[:pupil, pupil:] = imag
            right[pupil:, :pupil] = -imag
            right[pupil:, pupil:] = real
        t = jnp.dot(left[...], right[...], preferred_element_type=jnp.float32)
        for k in range(blocks):
            at = slice(k * rows, (k + 1) * rows)
            t_re, t_im = t[at, :pupil], t[at, pupil:]
            c_re, c_im = col_re[k : k + 1], col_im[k : k + 1]
            mid[at] = (t_re * c_re - t_im * c_im).astype(mid.dtype)
            mid[slice(half + k * rows, half + (k + 1) * rows)] = (t_re * c_im + t_im * c_re).astype(mid.dtype)
        d = jnp.dot(mid[...], second_ref[...], preferred_element_type=jnp.float32)
        if j == 0:
            own[...] = d
        else:
            term = (d * own[...]).reshape(2 * blocks, rows, d.shape[1])
            out_ref[:, j - 1, :] = jnp.sum(term, axis=0) * (2.0 * 4.0 / blocks)


def local(mod_points, pupil_mask, phase_offset, modes, block_map):
    count, height, pupil = modes.shape
    blocks = lax.axis_size("mod")
    length = 2 * pupil
    lanes = 128
    flat = modes.reshape(count, height, pupil // lanes, lanes).transpose(0, 2, 1, 3).reshape(-1, lanes)
    mark = jnp.broadcast_to(mod_points.astype(jnp.bfloat16)[:, None], (16, lanes))
    packed = jnp.concatenate([flat, mark], axis=0)
    spread = jnp.broadcast_to(packed[None], (blocks,) + packed.shape)
    gathered = lax.all_to_all(spread, "mod", 0, 0)

    mask = pupil_mask.astype(jnp.float32)
    field = jnp.stack([mask * jnp.cos(phase_offset), mask * jnp.sin(phase_offset)]).astype(jnp.bfloat16)[None]
    group = lax.axis_size("mode")
    for bit in ORDER:
        field = jnp.concatenate([field, lax.ppermute(field, "mode", [(i, i ^ bit) for i in range(group)])])

    table = sensor_table(length, pupil)
    rows = length // blocks
    ids = jnp.stack([lax.axis_index("mod"), lax.axis_index("mode")]).astype(jnp.int32)
    whole = lambda shape: pl.BlockSpec(shape, lambda i, m, d: (0,) * len(shape))
    return pl.pallas_call(
        tangent_kernel,
        grid_spec=pltpu.PrefetchScalarGridSpec(
            num_scalar_prefetch=2,
            grid=(1,),
            in_specs=[
                whole(gathered.shape),
                whole(field.shape),
                pl.BlockSpec((rows, pupil), lambda i, m, d: (m[d[0]], 0)),
                whole((pupil, length)),
            ],
            out_specs=whole((rows, count, length)),
            scratch_shapes=[
                pltpu.VMEM((length, length), jnp.bfloat16),
                pltpu.VMEM((pupil, length), jnp.bfloat16),
                pltpu.VMEM((length, length), jnp.bfloat16),
                pltpu.VMEM((2 * length, pupil), jnp.bfloat16),
                pltpu.VMEM((2 * length, length), jnp.float32),
            ],
        ),
        out_shape=jax.ShapeDtypeStruct((rows, count, length), jnp.float32),
        compiler_params=pltpu.CompilerParams(vmem_limit_bytes=40 * 2**20),
        cost_estimate=pl.CostEstimate(flops=2_700_000_000, bytes_accessed=2_000_000, transcendentals=0),
        name="tangent",
    )(block_map, ids, gathered, field, jnp.asarray(table, jnp.float32), jnp.asarray(table.T, jnp.bfloat16))


def solution(mesh):
    placed = (P("mod"), P("mode", None), P("mode", None), P("mode", "mod", None), P())
    return jax.shard_map(
        local, mesh=mesh, in_specs=placed, out_specs=P("mod", "mode", None), check_vma=False
    )
```

```python
import math

import jax
import jax.numpy as jnp
import numpy as np
from jax import lax
from jax.experimental import pallas as pl
from jax.experimental.pallas import tpu as pltpu
from jax.sharding import PartitionSpec as P

NPTS = 48
radius_cells = 6.0
ORDER = (8, 2, 4, 1)


def sensor_tables(length, pupil):
    c = np.arange(length) - length // 2
    n = np.arange(pupil) - pupil // 2
    s = c[:, None] + n[None, :]
    sign = np.where(c % 2 == 0, 1.0, -1.0)[:, None]
    with np.errstate(divide="ignore"):
        kernel = np.where(s % 2 != 0, sign * 2.0 / (length * np.cos(2.0 * np.pi * s / length)), 0.0)
    direct = np.where(np.abs(s % length - length // 2) == length // 4, 0.5, 0.0)
    place = (pupil - np.arange(pupil)) % pupil
    flip = np.zeros((pupil, pupil))
    flip[np.arange(pupil), place] = 1.0
    return kernel + direct, 2.0 * kernel[place].T, flip


def rotated(t_re, t_im, c_re, c_im):
    return t_re * c_re - t_im * c_im, t_re * c_im + t_im * c_re


def point_kernel(block_map, ids, field_ref, table_ref, left, columns, own, right):
    blocks = field_ref.shape[0]
    length, pupil = table_ref.shape
    rows = length // blocks
    height = pupil // blocks
    me = ids[1]
    points = []
    for place in range(blocks):
        other = sum(bit for t, bit in enumerate(ORDER) if place >> t & 1)
        at = pl.multiple_of((me ^ other) * height, height)
        part = field_ref[place]
        left[pl.ds(length + at, height), :pupil] = part[:height]
        left[pl.ds(length + at, height), pupil:] = part[height : 2 * height]
        points.append(part[2 * height :].astype(jnp.float32)[:1])
    theta = jnp.concatenate(points, axis=0) * (2.0 * math.pi / NPTS)
    scale = 2.0 * math.pi * radius_cells / length
    column = lax.broadcasted_iota(jnp.int32, (blocks, pupil), 1)
    odd = column % 2 == 1
    centred = (column - pupil // 2).astype(jnp.float32) * scale

    def factor(tilt):
        cos, sin = jnp.cos(tilt * centred), jnp.sin(tilt * centred)
        return jnp.where(odd, -sin, cos), jnp.where(odd, cos, sin)

    row_re, row_im = factor(jnp.cos(theta))
    col_re, col_im = factor(jnp.sin(theta))
    columns[0] = col_re
    columns[1] = col_im
    table = table_ref[pl.ds(pl.multiple_of(block_map[ids[0]] * rows, rows), rows), :]
    for k in range(blocks):
        at = slice(k * rows, (k + 1) * rows)
        left[at, :pupil] = (table * row_re[k : k + 1]).astype(left.dtype)
        left[at, pupil:] = (table * row_im[k : k + 1]).astype(left.dtype)
    re = left[length:, :pupil]
    im = left[length:, pupil:]
    right[:pupil, :pupil] = re
    right[:pupil, pupil:] = im
    right[pupil:, :pupil] = -im
    right[pupil:, pupil:] = re
    t = jnp.dot(left[:length], right[...], preferred_element_type=jnp.float32)
    half = blocks * rows
    weight = 4.0 / blocks / 2.0
    for k in range(blocks):
        at = slice(k * rows, (k + 1) * rows)
        low = slice(half + k * rows, half + (k + 1) * rows)
        u_re, u_im = rotated(t[at, :pupil], t[at, pupil:], col_re[k : k + 1], col_im[k : k + 1])
        own[at] = u_re * weight
        own[low] = u_im * weight


def mode_kernel(modes_ref, left, columns, own, mixing_ref, flip_ref, out_ref, other, right, mid, sums):
    count = out_ref.shape[1]
    _, blocks, pupil = columns.shape
    rows = out_ref.shape[0]
    half = blocks * rows
    re = left[half:, :pupil]
    im = left[half:, pupil:]
    other[...] = jnp.dot(own[...].astype(mid.dtype), mixing_ref[...], preferred_element_type=jnp.float32)
    for j in range(count):
        value = modes_ref[:, j].reshape(pupil, pupil)
        real = -value * im
        imag = value * re
        right[:pupil, :pupil] = real
        right[:pupil, pupil:] = imag
        right[pupil:, :pupil] = -imag
        right[pupil:, pupil:] = real
        t = jnp.dot(left[:half], right[...], preferred_element_type=jnp.float32)
        even = jnp.zeros((rows, pupil), jnp.float32)
        odd = jnp.zeros((rows, pupil), jnp.float32)
        for k in range(blocks):
            at = slice(k * rows, (k + 1) * rows)
            low = slice(half + k * rows, half + (k + 1) * rows)
            u_re, u_im = rotated(t[at, :pupil], t[at, pupil:], columns[0, k : k + 1], columns[1, k : k + 1])
            mid[at] = u_re.astype(mid.dtype)
            mid[low] = u_im.astype(mid.dtype)
            even += own[at] * u_re + own[low] * u_im
            odd += other[at] * u_re + other[low] * u_im
        d = jnp.dot(mid[...], mixing_ref[...], preferred_element_type=jnp.float32)
        for k in range(2 * blocks):
            at = slice(k * rows, (k + 1) * rows)
            even += other[at] * d[at]
            odd += own[at] * d[at]
        sums[2 * j * rows : (2 * j + 1) * rows] = even + odd
        sums[(2 * j + 1) * rows : (2 * j + 2) * rows] = even - odd
    total = sums[...]
    high = total.astype(jnp.bfloat16)
    low = (total - high.astype(jnp.float32)).astype(jnp.bfloat16)
    flip = flip_ref[...]
    placed = jnp.dot(high, flip, preferred_element_type=jnp.float32) + jnp.dot(low, flip, preferred_element_type=jnp.float32)
    for j in range(count):
        out_ref[:, j, :pupil] = placed[2 * j * rows : (2 * j + 1) * rows]
        out_ref[:, j, pupil:] = placed[(2 * j + 1) * rows : (2 * j + 2) * rows]


def local(mod_points, pupil_mask, phase_offset, modes, block_map):
    count, height, pupil = modes.shape
    blocks = lax.axis_size("mod")
    group = lax.axis_size("mode")
    length = 2 * pupil
    rows = length // blocks
    gathered = lax.all_to_all(jnp.broadcast_to(modes[None], (blocks,) + modes.shape), "mod", 0, 0)

    point = jnp.broadcast_to(mod_points.astype(jnp.bfloat16)[:, None], (8, pupil))
    swap = [(b * group + g, g * group + b) for b in range(blocks) for g in range(group)]
    point = lax.ppermute(point, ("mod", "mode"), swap)
    mask = pupil_mask.astype(jnp.float32)
    field = jnp.concatenate([mask * jnp.cos(phase_offset), mask * jnp.sin(phase_offset)]).astype(jnp.bfloat16)
    field = jnp.concatenate([field, point])[None]
    for bit in ORDER:
        field = jnp.concatenate([field, lax.ppermute(field, "mode", [(i, i ^ bit) for i in range(group)])])

    table, mixing, flip = sensor_tables(length, pupil)
    table = jnp.asarray(table, jnp.float32)
    mixing = jnp.asarray(mixing, jnp.bfloat16)
    flip = jnp.asarray(flip, jnp.bfloat16)
    ids = jnp.stack([lax.axis_index("mod"), lax.axis_index("mode")]).astype(jnp.int32)
    vmem = pl.BlockSpec(memory_space=pltpu.VMEM)
    smem = pl.BlockSpec(memory_space=pltpu.SMEM)
    limit = pltpu.CompilerParams(vmem_limit_bytes=12 * 2**20)
    left, columns, own = pl.pallas_call(
        point_kernel,
        in_specs=[smem, smem, vmem, vmem],
        out_specs=[vmem] * 3,
        out_shape=[
            jax.ShapeDtypeStruct((length + pupil, length), jnp.bfloat16),
            jax.ShapeDtypeStruct((2, blocks, pupil), jnp.float32),
            jax.ShapeDtypeStruct((2 * length, pupil), jnp.float32),
        ],
        scratch_shapes=[pltpu.VMEM((length, length), jnp.bfloat16)],
        compiler_params=limit,
        cost_estimate=pl.CostEstimate(flops=400_000_000, bytes_accessed=4_000_000, transcendentals=0),
        name="point",
    )(block_map, ids, field, table)
    return pl.pallas_call(
        mode_kernel,
        in_specs=[vmem] * 6,
        out_specs=vmem,
        out_shape=jax.ShapeDtypeStruct((rows, count, length), jnp.float32),
        scratch_shapes=[
            pltpu.VMEM((2 * length, pupil), jnp.float32),
            pltpu.VMEM((length, length), jnp.bfloat16),
            pltpu.VMEM((2 * length, pupil), jnp.bfloat16),
            pltpu.VMEM((2 * count * rows, pupil), jnp.float32),
        ],
        compiler_params=limit,
        cost_estimate=pl.CostEstimate(flops=1_700_000_000, bytes_accessed=5_000_000, transcendentals=0),
        name="tangent",
    )(gathered, left, columns, own, mixing, flip)


def solution(mesh):
    placed = (P("mod"), P("mode", None), P("mode", None), P("mode", "mod", None), P())
    return jax.shard_map(
        local, mesh=mesh, in_specs=placed, out_specs=P("mod", "mode", None), check_vma=False
    )
```

```python
import math

import jax
import jax.numpy as jnp
import numpy as np
from jax import lax
from jax.experimental import pallas as pl
from jax.experimental.pallas import tpu as pltpu
from jax.sharding import PartitionSpec as P

NPTS = 48
radius_cells = 6.0


def peer_order(blocks):
    return [2 * (i % (blocks // 2)) + i // (blocks // 2) for i in range(blocks)]


def sensor_table(length, pupil):
    c = np.arange(length) - length // 2
    n = np.arange(pupil) - pupil // 2
    s = c[:, None] + n[None, :]
    odd = s % 2 != 0
    with np.errstate(divide="ignore"):
        kernel = 2.0 / (length * np.cos(2.0 * np.pi * s / length))
    shift = np.abs(s % length - length // 2) == length // 4
    direct = np.where(shift, np.where(n % 2 == 0, 0.5, -0.5)[None, :], 0.0)
    return np.where(odd, kernel, direct)


def tangent_kernel(block_map, ids, modes_ref, near_ref, far_ref, table_ref, second_ref, out_ref, left, base, right, own):
    blocks = modes_ref.shape[0]
    length, pupil = table_ref.shape
    rows = length // blocks
    height = pupil // blocks
    count = out_ref.shape[1]
    half_group = blocks // 2
    for place in range(blocks):
        core, chip = divmod(place, half_group)
        part = (near_ref, far_ref)[core][chip]
        block = ids[1] ^ (2 * chip + core)
        at = pl.multiple_of(((block & 1) * half_group + (block >> 1)) * height, height)
        base[pl.ds(at, height), :pupil] = part[:height]
        base[pl.ds(at, height), pupil:] = part[height:]
    point = jnp.concatenate([modes_ref[i][count * height :].astype(jnp.float32)[:1] for i in range(blocks)], axis=0)
    theta = point * (2.0 * math.pi / NPTS)
    scale = 2.0 * math.pi * radius_cells / length
    place = lax.broadcasted_iota(jnp.int32, (blocks, pupil), 1)
    odd = (place & 1) == 1
    block = place // height
    row = (2 * (block % half_group) + block // half_group) * height + place % height

    def factor(tilt, index):
        angle = tilt * ((index - pupil // 2).astype(jnp.float32) * scale)
        cos, sin = jnp.cos(angle), jnp.sin(angle)
        return jnp.where(odd, -sin, cos), jnp.where(odd, cos, sin)

    row_re, row_im = factor(jnp.cos(theta), row)
    col_re, col_im = factor(jnp.sin(theta), place)
    table = table_ref[pl.ds(pl.multiple_of(block_map[ids[0]] * rows, rows), rows), :]
    for k in range(blocks):
        at = slice(k * rows, (k + 1) * rows)
        left[at, :pupil] = (table * row_re[k : k + 1]).astype(left.dtype)
        left[at, pupil:] = (table * row_im[k : k + 1]).astype(left.dtype)

    def first(j):
        real = base[:, :pupil]
        imag = base[:, pupil:]
        if j >= 0:
            value = modes_ref[:, j * height : (j + 1) * height].reshape(pupil, pupil)
            real, imag = -value * imag, value * real
        slot = right.at[j % 2]
        slot[:pupil, :pupil] = real
        slot[:pupil, pupil:] = imag
        slot[pupil:, :pupil] = -imag
        slot[pupil:, pupil:] = real
        return jnp.dot(left[...], slot[...], preferred_element_type=jnp.float32)

    def second(t):
        parts = ([], [])
        for k in range(blocks):
            t_re, t_im = t[k * rows : (k + 1) * rows, :pupil], t[k * rows : (k + 1) * rows, pupil:]
            c_re, c_im = col_re[k : k + 1], col_im[k : k + 1]
            parts[0].append(t_re * c_re - t_im * c_im)
            parts[1].append(t_re * c_im + t_im * c_re)
        mixed = jnp.concatenate(parts[0] + parts[1], axis=0).astype(jnp.bfloat16)
        return jnp.dot(mixed, second_ref[...], preferred_element_type=jnp.float32)

    def third(j, d):
        if j < 0:
            own[...] = d * (2.0 * 4.0 / blocks)
            return
        total = jnp.zeros((rows, length), jnp.float32)
        for k in range(2 * blocks):
            at = slice(k * rows, (k + 1) * rows)
            total += own[at] * d[at]
        out_ref[:, j, :] = total

    firsts, seconds = {}, {}
    for step in range(count + 3):
        if step <= count:
            firsts[step] = first(step - 1)
        if 0 <= step - 1 <= count:
            seconds[step - 1] = second(firsts.pop(step - 1))
        if 0 <= step - 2 <= count:
            third(step - 3, seconds.pop(step - 2))


def local(mod_points, pupil_mask, phase_offset, modes, block_map):
    count, height, pupil = modes.shape
    blocks = lax.axis_size("mod")
    group = lax.axis_size("mode")
    length = 2 * pupil
    rows = length // blocks
    order = peer_order(blocks)
    mark = jnp.broadcast_to(mod_points.astype(jnp.bfloat16)[:, None], (8, pupil))
    packed = jnp.concatenate([modes.reshape(count * height, pupil), mark])
    spread = jnp.broadcast_to(packed[None], (blocks,) + packed.shape)
    gathered = lax.all_to_all(spread, "mod", 0, 0, axis_index_groups=[order])

    mask = pupil_mask.astype(jnp.float32)
    field = jnp.concatenate([mask * jnp.cos(phase_offset), mask * jnp.sin(phase_offset)]).astype(jnp.bfloat16)
    swap = lambda x, bit: lax.ppermute(x, "mode", [(i, i ^ bit) for i in range(group)])
    near = jnp.stack([field] + [swap(field, 2 * t) for t in range(1, group // 2)])
    far = swap(near, 1)

    table = sensor_table(length, pupil)
    places = np.concatenate([np.arange(height) + b * height for b in order])
    ids = jnp.stack([lax.axis_index("mod"), lax.axis_index("mode")]).astype(jnp.int32)
    vmem = pl.BlockSpec(memory_space=pltpu.VMEM)
    smem = pl.BlockSpec(memory_space=pltpu.SMEM)
    return pl.pallas_call(
        tangent_kernel,
        in_specs=[smem, smem] + [vmem] * 5,
        out_specs=vmem,
        out_shape=jax.ShapeDtypeStruct((rows, count, length), jnp.float32),
        scratch_shapes=[
            pltpu.VMEM((length, length), jnp.bfloat16),
            pltpu.VMEM((pupil, length), jnp.bfloat16),
            pltpu.VMEM((2, length, length), jnp.bfloat16),
            pltpu.VMEM((2 * length, length), jnp.float32),
        ],
        compiler_params=pltpu.CompilerParams(vmem_limit_bytes=24 * 2**20),
        cost_estimate=pl.CostEstimate(flops=2_700_000_000, bytes_accessed=2_000_000, transcendentals=0),
        name="tangent",
    )(
        block_map,
        ids,
        gathered,
        near,
        far,
        jnp.asarray(table[:, places], jnp.float32),
        jnp.asarray(table.T, jnp.bfloat16),
    )


def solution(mesh):
    placed = (P("mod"), P("mode", None), P("mode", None), P("mode", "mod", None), P())
    return jax.shard_map(
        local, mesh=mesh, in_specs=placed, out_specs=P("mod", "mode", None), check_vma=False
    )
```

```python
import math

import jax
import jax.numpy as jnp
import numpy as np
from jax import lax
from jax.experimental import pallas as pl
from jax.experimental.pallas import tpu as pltpu
from jax.sharding import PartitionSpec as P

NPTS = 48
radius_cells = 6.0


def peer_order(blocks):
    return [2 * (i % (blocks // 2)) + i // (blocks // 2) for i in range(blocks)]


def sensor_table(length, pupil):
    c = np.arange(length) - length // 2
    n = np.arange(pupil) - pupil // 2
    s = c[:, None] + n[None, :]
    odd = s % 2 != 0
    with np.errstate(divide="ignore"):
        kernel = 2.0 / (length * np.cos(2.0 * np.pi * s / length))
    shift = np.abs(s % length - length // 2) == length // 4
    direct = np.where(shift, np.where(n % 2 == 0, 0.5, -0.5)[None, :], 0.0)
    return np.where(odd, kernel, direct)


def tangent_kernel(block_map, ids, modes_ref, pair_ref, near_ref, fourth_ref, far_ref, table_ref, second_ref, out_ref, left, base, right, own):
    blocks = modes_ref.shape[0]
    length, pupil = table_ref.shape
    rows = length // blocks
    height = pupil // blocks
    count = out_ref.shape[1]
    half_group = blocks // 2
    me = ids[1]
    core = me & 1
    found = []
    for r in range(2):
        found.append((pair_ref[r], me ^ r))
        found.append((fourth_ref[r], me ^ (8 + r)))
        for i in range(3):
            found.append((near_ref[i, r], me ^ (2 * (i + 1 + 4 * core) + r)))
            found.append((far_ref[i, r], me ^ (2 * (i + 5 - 4 * core) + 1 - r)))
    for part, block in found:
        at = pl.multiple_of(((block & 1) * half_group + (block >> 1)) * height, height)
        base[pl.ds(at, height), :pupil] = part[:height]
        base[pl.ds(at, height), pupil:] = part[height:]
    point = jnp.concatenate([modes_ref[i][count * height :].astype(jnp.float32)[:1] for i in range(blocks)], axis=0)
    theta = point * (2.0 * math.pi / NPTS)
    scale = 2.0 * math.pi * radius_cells / length
    place = lax.broadcasted_iota(jnp.int32, (blocks, pupil), 1)
    odd = (place & 1) == 1
    block = place // height
    row = (2 * (block % half_group) + block // half_group) * height + place % height

    def factor(tilt, index):
        angle = tilt * ((index - pupil // 2).astype(jnp.float32) * scale)
        cos, sin = jnp.cos(angle), jnp.sin(angle)
        return jnp.where(odd, -sin, cos), jnp.where(odd, cos, sin)

    row_re, row_im = factor(jnp.cos(theta), row)
    col_re, col_im = factor(jnp.sin(theta), place)
    table = table_ref[pl.ds(pl.multiple_of(block_map[ids[0]] * rows, rows), rows), :]
    for k in range(blocks):
        at = slice(k * rows, (k + 1) * rows)
        left[at, :pupil] = (table * row_re[k : k + 1]).astype(left.dtype)
        left[at, pupil:] = (table * row_im[k : k + 1]).astype(left.dtype)

    def first(j):
        real = base[:, :pupil]
        imag = base[:, pupil:]
        if j >= 0:
            value = modes_ref[:, j * height : (j + 1) * height].reshape(pupil, pupil)
            real, imag = -value * imag, value * real
        slot = right.at[j % 2]
        slot[:pupil, :pupil] = real
        slot[:pupil, pupil:] = imag
        slot[pupil:, :pupil] = -imag
        slot[pupil:, pupil:] = real
        return jnp.dot(left[...], slot[...], preferred_element_type=jnp.float32)

    def second(t):
        parts = ([], [])
        for k in range(blocks):
            t_re, t_im = t[k * rows : (k + 1) * rows, :pupil], t[k * rows : (k + 1) * rows, pupil:]
            c_re, c_im = col_re[k : k + 1], col_im[k : k + 1]
            parts[0].append(t_re * c_re - t_im * c_im)
            parts[1].append(t_re * c_im + t_im * c_re)
        mixed = jnp.concatenate(parts[0] + parts[1], axis=0).astype(jnp.bfloat16)
        return jnp.dot(mixed, second_ref[...], preferred_element_type=jnp.float32)

    def third(j, d):
        if j < 0:
            own[...] = d * (2.0 * 4.0 / blocks)
            return
        total = jnp.zeros((rows, length), jnp.float32)
        for k in range(2 * blocks):
            at = slice(k * rows, (k + 1) * rows)
            total += own[at] * d[at]
        out_ref[:, j, :] = total

    firsts, seconds = {}, {}
    for step in range(count + 3):
        if step <= count:
            firsts[step] = first(step - 1)
        if 0 <= step - 1 <= count:
            seconds[step - 1] = second(firsts.pop(step - 1))
        if 0 <= step - 2 <= count:
            third(step - 3, seconds.pop(step - 2))


def local(mod_points, pupil_mask, phase_offset, modes, block_map):
    count, height, pupil = modes.shape
    blocks = lax.axis_size("mod")
    group = lax.axis_size("mode")
    length = 2 * pupil
    rows = length // blocks
    order = peer_order(blocks)
    mark = jnp.broadcast_to(mod_points.astype(jnp.bfloat16)[:, None], (8, pupil))
    packed = jnp.concatenate([modes.reshape(count * height, pupil), mark])
    spread = jnp.broadcast_to(packed[None], (blocks,) + packed.shape)
    gathered = lax.all_to_all(spread, "mod", 0, 0, axis_index_groups=[order])

    mask = pupil_mask.astype(jnp.float32)
    field = jnp.concatenate([mask * jnp.cos(phase_offset), mask * jnp.sin(phase_offset)]).astype(jnp.bfloat16)
    pairs = lambda t0, t1: [(i, i ^ (2 * (t1 if i & 1 else t0))) for i in range(group)]
    cores = [(i, i ^ 1) for i in range(group)]
    pair = jnp.stack([field, lax.ppermute(field, "mode", cores)])
    near = jnp.stack([lax.ppermute(pair, "mode", pairs(t, t + 4)) for t in range(1, 4)])
    fourth = lax.ppermute(pair, "mode", pairs(4, 4))
    far = lax.ppermute(near, "mode", cores)

    table = sensor_table(length, pupil)
    places = np.concatenate([np.arange(height) + b * height for b in order])
    ids = jnp.stack([lax.axis_index("mod"), lax.axis_index("mode")]).astype(jnp.int32)
    vmem = pl.BlockSpec(memory_space=pltpu.VMEM)
    smem = pl.BlockSpec(memory_space=pltpu.SMEM)
    return pl.pallas_call(
        tangent_kernel,
        in_specs=[smem, smem] + [vmem] * 7,
        out_specs=vmem,
        out_shape=jax.ShapeDtypeStruct((rows, count, length), jnp.float32),
        scratch_shapes=[
            pltpu.VMEM((length, length), jnp.bfloat16),
            pltpu.VMEM((pupil, length), jnp.bfloat16),
            pltpu.VMEM((2, length, length), jnp.bfloat16),
            pltpu.VMEM((2 * length, length), jnp.float32),
        ],
        compiler_params=pltpu.CompilerParams(vmem_limit_bytes=24 * 2**20),
        cost_estimate=pl.CostEstimate(flops=2_700_000_000, bytes_accessed=2_000_000, transcendentals=0),
        name="tangent",
    )(
        block_map,
        ids,
        gathered,
        pair,
        near,
        fourth,
        far,
        jnp.asarray(table[:, places], jnp.float32),
        jnp.asarray(table.T, jnp.bfloat16),
    )


def solution(mesh):
    placed = (P("mod"), P("mode", None), P("mode", None), P("mode", "mod", None), P())
    return jax.shard_map(
        local, mesh=mesh, in_specs=placed, out_specs=P("mod", "mode", None), check_vma=False
    )
```

```python
import math

import jax
import jax.numpy as jnp
import numpy as np
from jax import lax
from jax.experimental import pallas as pl
from jax.experimental.pallas import tpu as pltpu
from jax.sharding import PartitionSpec as P

NPTS = 48
radius_cells = 6.0


def peer_order(blocks):
    chips = blocks // 2
    line = [i // 2 if i % 2 == 0 else chips - 1 - i // 2 for i in range(chips)]
    return [2 * z + y for y in range(2) for z in line]


def sensor_table(length, pupil):
    c = np.arange(length) - length // 2
    n = np.arange(pupil) - pupil // 2
    s = c[:, None] + n[None, :]
    odd = s % 2 != 0
    with np.errstate(divide="ignore"):
        kernel = 2.0 / (length * np.cos(2.0 * np.pi * s / length))
    shift = np.abs(s % length - length // 2) == length // 4
    direct = np.where(shift, np.where(n % 2 == 0, 0.5, -0.5)[None, :], 0.0)
    return np.where(odd, kernel, direct)


def tangent_kernel(block_map, ids, modes_ref, pair_ref, near_ref, fourth_ref, far_ref, table_ref, second_ref, out_ref, left, base, right, own):
    blocks = modes_ref.shape[0]
    length, pupil = table_ref.shape
    rows = length // blocks
    height = pupil // blocks
    count = out_ref.shape[1]
    half_group = blocks // 2
    me = ids[1]
    core = me & 1
    found = []
    for r in range(2):
        found.append((pair_ref[r], me ^ r))
        found.append((fourth_ref[r], me ^ (8 + r)))
        for i in range(3):
            found.append((near_ref[i, r], me ^ (2 * (i + 1 + 4 * core) + r)))
            found.append((far_ref[i, r], me ^ (2 * (i + 5 - 4 * core) + 1 - r)))
    for part, block in found:
        chip = block >> 1
        chip = jnp.where(chip < half_group // 2, 2 * chip, 2 * half_group - 1 - 2 * chip)
        at = pl.multiple_of(((block & 1) * half_group + chip) * height, height)
        base[pl.ds(at, height), :pupil] = part[:height]
        base[pl.ds(at, height), pupil:] = part[height:]
    point = jnp.concatenate([modes_ref[i][count * height :].astype(jnp.float32)[:1] for i in range(blocks)], axis=0)
    theta = point * (2.0 * math.pi / NPTS)
    scale = 2.0 * math.pi * radius_cells / length
    place = lax.broadcasted_iota(jnp.int32, (blocks, pupil), 1)
    odd = (place & 1) == 1
    block = place // height
    chip = block % half_group
    chip = jnp.where(chip % 2 == 0, chip // 2, half_group - 1 - chip // 2)
    row = (2 * chip + block // half_group) * height + place % height

    def factor(tilt, index):
        angle = tilt * ((index - pupil // 2).astype(jnp.float32) * scale)
        cos, sin = jnp.cos(angle), jnp.sin(angle)
        return jnp.where(odd, -sin, cos), jnp.where(odd, cos, sin)

    row_re, row_im = factor(jnp.cos(theta), row)
    col_re, col_im = factor(jnp.sin(theta), place)
    table = table_ref[pl.ds(pl.multiple_of(block_map[ids[0]] * rows, rows), rows), :]
    for k in range(blocks):
        at = slice(k * rows, (k + 1) * rows)
        left[at, :pupil] = (table * row_re[k : k + 1]).astype(left.dtype)
        left[at, pupil:] = (table * row_im[k : k + 1]).astype(left.dtype)

    def first(j):
        real = base[:, :pupil]
        imag = base[:, pupil:]
        if j >= 0:
            value = modes_ref[:, j * height : (j + 1) * height].reshape(pupil, pupil)
            real, imag = -value * imag, value * real
        slot = right.at[j % 2]
        slot[:pupil, :pupil] = real
        slot[:pupil, pupil:] = imag
        slot[pupil:, :pupil] = -imag
        slot[pupil:, pupil:] = real
        return jnp.dot(left[...], slot[...], preferred_element_type=jnp.float32)

    def second(t):
        parts = ([], [])
        for k in range(blocks):
            t_re, t_im = t[k * rows : (k + 1) * rows, :pupil], t[k * rows : (k + 1) * rows, pupil:]
            c_re, c_im = col_re[k : k + 1], col_im[k : k + 1]
            parts[0].append(t_re * c_re - t_im * c_im)
            parts[1].append(t_re * c_im + t_im * c_re)
        mixed = jnp.concatenate(parts[0] + parts[1], axis=0).astype(jnp.bfloat16)
        return jnp.dot(mixed, second_ref[...], preferred_element_type=jnp.float32)

    def third(j, d):
        if j < 0:
            own[...] = d * (2.0 * 4.0 / blocks)
            return
        total = jnp.zeros((rows, length), jnp.float32)
        for k in range(2 * blocks):
            at = slice(k * rows, (k + 1) * rows)
            total += own[at] * d[at]
        out_ref[:, j, :] = total

    firsts, seconds = {}, {}
    for step in range(count + 3):
        if step <= count:
            firsts[step] = first(step - 1)
        if 0 <= step - 1 <= count:
            seconds[step - 1] = second(firsts.pop(step - 1))
        if 0 <= step - 2 <= count:
            third(step - 3, seconds.pop(step - 2))


def local(mod_points, pupil_mask, phase_offset, modes, block_map):
    count, height, pupil = modes.shape
    blocks = lax.axis_size("mod")
    group = lax.axis_size("mode")
    length = 2 * pupil
    rows = length // blocks
    order = peer_order(blocks)
    mark = jnp.broadcast_to(mod_points.astype(jnp.bfloat16)[:, None], (8, pupil))
    packed = jnp.concatenate([modes.reshape(count * height, pupil), mark])
    spread = jnp.broadcast_to(packed[None], (blocks,) + packed.shape)
    gathered = lax.all_to_all(spread, "mod", 0, 0, axis_index_groups=[order])

    mask = pupil_mask.astype(jnp.float32)
    field = jnp.concatenate([mask * jnp.cos(phase_offset), mask * jnp.sin(phase_offset)]).astype(jnp.bfloat16)
    pairs = lambda t0, t1: [(i, i ^ (2 * (t1 if i & 1 else t0))) for i in range(group)]
    cores = [(i, i ^ 1) for i in range(group)]
    pair = jnp.stack([field, lax.ppermute(field, "mode", cores)])
    near = jnp.stack([lax.ppermute(pair, "mode", pairs(t, t + 4)) for t in range(1, 4)])
    fourth = lax.ppermute(pair, "mode", pairs(4, 4))
    far = lax.ppermute(near, "mode", cores)

    table = sensor_table(length, pupil)
    places = np.concatenate([np.arange(height) + b * height for b in order])
    ids = jnp.stack([lax.axis_index("mod"), lax.axis_index("mode")]).astype(jnp.int32)
    vmem = pl.BlockSpec(memory_space=pltpu.VMEM)
    smem = pl.BlockSpec(memory_space=pltpu.SMEM)
    return pl.pallas_call(
        tangent_kernel,
        in_specs=[smem, smem] + [vmem] * 7,
        out_specs=vmem,
        out_shape=jax.ShapeDtypeStruct((rows, count, length), jnp.float32),
        scratch_shapes=[
            pltpu.VMEM((length, length), jnp.bfloat16),
            pltpu.VMEM((pupil, length), jnp.bfloat16),
            pltpu.VMEM((2, length, length), jnp.bfloat16),
            pltpu.VMEM((2 * length, length), jnp.float32),
        ],
        compiler_params=pltpu.CompilerParams(vmem_limit_bytes=24 * 2**20),
        cost_estimate=pl.CostEstimate(flops=2_700_000_000, bytes_accessed=2_000_000, transcendentals=0),
        name="tangent",
    )(
        block_map,
        ids,
        gathered,
        pair,
        near,
        fourth,
        far,
        jnp.asarray(table[:, places], jnp.float32),
        jnp.asarray(table.T, jnp.bfloat16),
    )


def solution(mesh):
    placed = (P("mod"), P("mode", None), P("mode", None), P("mode", "mod", None), P())
    return jax.shard_map(
        local, mesh=mesh, in_specs=placed, out_specs=P("mod", "mode", None), check_vma=False
    )
```

```python
import math

import jax
import jax.numpy as jnp
import numpy as np
from jax import lax
from jax.experimental import pallas as pl
from jax.experimental.pallas import tpu as pltpu
from jax.sharding import PartitionSpec as P

NPTS = 48
radius_cells = 6.0


def peer_order(blocks):
    return [2 * (i % (blocks // 2)) + i // (blocks // 2) for i in range(blocks)]


def sensor_table(length, pupil):
    c = np.arange(length) - length // 2
    n = np.arange(pupil) - pupil // 2
    s = c[:, None] + n[None, :]
    odd = s % 2 != 0
    with np.errstate(divide="ignore"):
        kernel = 2.0 / (length * np.cos(2.0 * np.pi * s / length))
    shift = np.abs(s % length - length // 2) == length // 4
    direct = np.where(shift, np.where(n % 2 == 0, 0.5, -0.5)[None, :], 0.0)
    return np.where(odd, kernel, direct)


def tangent_kernel(block_map, ids, modes_ref, pair_ref, near_ref, fourth_ref, far_ref, table_ref, second_ref, out_ref, left, base, right, own):
    blocks = modes_ref.shape[0]
    length, pupil = table_ref.shape
    rows = length // blocks
    height = pupil // blocks
    count = out_ref.shape[1]
    half_group = blocks // 2
    me = ids[1]
    core = me & 1
    found = []
    for r in range(2):
        found.append((pair_ref[r], me ^ r))
        found.append((fourth_ref[r], me ^ (8 + r)))
        for i in range(3):
            found.append((near_ref[i, r], me ^ (2 * (i + 5 - 4 * core) + r)))
            found.append((far_ref[i, r], me ^ (2 * (i + 1 + 4 * core) + 1 - r)))
    for part, block in found:
        at = pl.multiple_of(((block & 1) * half_group + (block >> 1)) * height, height)
        base[pl.ds(at, height), :pupil] = part[:height]
        base[pl.ds(at, height), pupil:] = part[height:]
    point = jnp.concatenate([modes_ref[i][count * height :].astype(jnp.float32)[:1] for i in range(blocks)], axis=0)
    theta = point * (2.0 * math.pi / NPTS)
    scale = 2.0 * math.pi * radius_cells / length
    place = lax.broadcasted_iota(jnp.int32, (blocks, pupil), 1)
    odd = (place & 1) == 1
    block = place // height
    row = (2 * (block % half_group) + block // half_group) * height + place % height

    def factor(tilt, index):
        angle = tilt * ((index - pupil // 2).astype(jnp.float32) * scale)
        cos, sin = jnp.cos(angle), jnp.sin(angle)
        return jnp.where(odd, -sin, cos), jnp.where(odd, cos, sin)

    row_re, row_im = factor(jnp.cos(theta), row)
    col_re, col_im = factor(jnp.sin(theta), place)
    table = table_ref[pl.ds(pl.multiple_of(block_map[ids[0]] * rows, rows), rows), :]
    for k in range(blocks):
        at = slice(k * rows, (k + 1) * rows)
        left[at, :pupil] = (table * row_re[k : k + 1]).astype(left.dtype)
        left[at, pupil:] = (table * row_im[k : k + 1]).astype(left.dtype)

    def first(j):
        real = base[:, :pupil]
        imag = base[:, pupil:]
        if j >= 0:
            value = modes_ref[:, j * height : (j + 1) * height].reshape(pupil, pupil)
            real, imag = -value * imag, value * real
        slot = right.at[j % 2]
        slot[:pupil, :pupil] = real
        slot[:pupil, pupil:] = imag
        slot[pupil:, :pupil] = -imag
        slot[pupil:, pupil:] = real
        return jnp.dot(left[...], slot[...], preferred_element_type=jnp.float32)

    def second(t):
        parts = ([], [])
        for k in range(blocks):
            t_re, t_im = t[k * rows : (k + 1) * rows, :pupil], t[k * rows : (k + 1) * rows, pupil:]
            c_re, c_im = col_re[k : k + 1], col_im[k : k + 1]
            parts[0].append(t_re * c_re - t_im * c_im)
            parts[1].append(t_re * c_im + t_im * c_re)
        mixed = jnp.concatenate(parts[0] + parts[1], axis=0).astype(jnp.bfloat16)
        return jnp.dot(mixed, second_ref[...], preferred_element_type=jnp.float32)

    def third(j, d):
        if j < 0:
            own[...] = d * (2.0 * 4.0 / blocks)
            return
        total = jnp.zeros((rows, length), jnp.float32)
        for k in range(2 * blocks):
            at = slice(k * rows, (k + 1) * rows)
            total += own[at] * d[at]
        out_ref[:, j, :] = total

    firsts, seconds = {}, {}
    for step in range(count + 3):
        if step <= count:
            firsts[step] = first(step - 1)
        if 0 <= step - 1 <= count:
            seconds[step - 1] = second(firsts.pop(step - 1))
        if 0 <= step - 2 <= count:
            third(step - 3, seconds.pop(step - 2))


def local(mod_points, pupil_mask, phase_offset, modes, block_map):
    count, height, pupil = modes.shape
    blocks = lax.axis_size("mod")
    group = lax.axis_size("mode")
    length = 2 * pupil
    rows = length // blocks
    order = peer_order(blocks)
    mark = jnp.broadcast_to(mod_points.astype(jnp.bfloat16)[:, None], (8, pupil))
    packed = jnp.concatenate([modes.reshape(count * height, pupil), mark])
    spread = jnp.broadcast_to(packed[None], (blocks,) + packed.shape)
    gathered = lax.all_to_all(spread, "mod", 0, 0, axis_index_groups=[order])

    mask = pupil_mask.astype(jnp.float32)
    field = jnp.concatenate([mask * jnp.cos(phase_offset), mask * jnp.sin(phase_offset)]).astype(jnp.bfloat16)
    pairs = lambda t0, t1: [(i, i ^ (2 * (t1 if i & 1 else t0))) for i in range(group)]
    cores = [(i, i ^ 1) for i in range(group)]
    pair = jnp.stack([field, lax.ppermute(field, "mode", cores)])
    near = jnp.stack([lax.ppermute(pair, "mode", pairs(t + 4, t)) for t in range(1, 4)])
    fourth = lax.ppermute(pair, "mode", pairs(4, 4))
    far = lax.ppermute(near, "mode", cores)

    table = sensor_table(length, pupil)
    places = np.concatenate([np.arange(height) + b * height for b in order])
    ids = jnp.stack([lax.axis_index("mod"), lax.axis_index("mode")]).astype(jnp.int32)
    vmem = pl.BlockSpec(memory_space=pltpu.VMEM)
    smem = pl.BlockSpec(memory_space=pltpu.SMEM)
    return pl.pallas_call(
        tangent_kernel,
        in_specs=[smem, smem] + [vmem] * 7,
        out_specs=vmem,
        out_shape=jax.ShapeDtypeStruct((rows, count, length), jnp.float32),
        scratch_shapes=[
            pltpu.VMEM((length, length), jnp.bfloat16),
            pltpu.VMEM((pupil, length), jnp.bfloat16),
            pltpu.VMEM((2, length, length), jnp.bfloat16),
            pltpu.VMEM((2 * length, length), jnp.float32),
        ],
        compiler_params=pltpu.CompilerParams(vmem_limit_bytes=24 * 2**20),
        cost_estimate=pl.CostEstimate(flops=2_700_000_000, bytes_accessed=2_000_000, transcendentals=0),
        name="tangent",
    )(
        block_map,
        ids,
        gathered,
        pair,
        near,
        fourth,
        far,
        jnp.asarray(table[:, places], jnp.float32),
        jnp.asarray(table.T, jnp.bfloat16),
    )


def solution(mesh):
    placed = (P("mod"), P("mode", None), P("mode", None), P("mode", "mod", None), P())
    return jax.shard_map(
        local, mesh=mesh, in_specs=placed, out_specs=P("mod", "mode", None), check_vma=False
    )
```

```python
import math

import jax
import jax.numpy as jnp
import numpy as np
from jax import lax
from jax.experimental import pallas as pl
from jax.experimental.pallas import tpu as pltpu
from jax.sharding import PartitionSpec as P

NPTS = 48
radius_cells = 6.0


def sensor_table(length, pupil):
    c = np.arange(length) - length // 2
    n = np.arange(pupil) - pupil // 2
    s = c[:, None] + n[None, :]
    odd = s % 2 != 0
    with np.errstate(divide="ignore"):
        kernel = 2.0 / (length * np.cos(2.0 * np.pi * s / length))
    shift = np.abs(s % length - length // 2) == length // 4
    direct = np.where(shift, np.where(n % 2 == 0, 0.5, -0.5)[None, :], 0.0)
    return np.where(odd, kernel, direct)


def tangent_kernel(block_map, ids, modes_ref, pair_ref, near_ref, fourth_ref, far_ref, table_ref, second_ref, out_ref, left, base, right, own):
    blocks = modes_ref.shape[0]
    length, pupil = table_ref.shape
    rows = length // blocks
    height = pupil // blocks
    count = out_ref.shape[1]
    me = ids[1]
    core = me & 1
    found = []
    for r in range(2):
        found.append((pair_ref[r], me ^ r))
        found.append((fourth_ref[r], me ^ (8 + r)))
        for i in range(3):
            found.append((near_ref[i, r], me ^ (2 * (i + 1 + 4 * core) + r)))
            found.append((far_ref[i, r], me ^ (2 * (i + 5 - 4 * core) + 1 - r)))
    for part, block in found:
        at = pl.multiple_of(block * height, height)
        base[pl.ds(at, height), :pupil] = part[:height]
        base[pl.ds(at, height), pupil:] = part[height:]
    point = jnp.concatenate([modes_ref[i][count * height :].astype(jnp.float32)[:1] for i in range(blocks)], axis=0)
    theta = point * (2.0 * math.pi / NPTS)
    scale = 2.0 * math.pi * radius_cells / length
    place = lax.broadcasted_iota(jnp.int32, (blocks, pupil), 1)
    odd = (place & 1) == 1

    def factor(tilt):
        angle = tilt * ((place - pupil // 2).astype(jnp.float32) * scale)
        cos, sin = jnp.cos(angle), jnp.sin(angle)
        return jnp.where(odd, -sin, cos), jnp.where(odd, cos, sin)

    row_re, row_im = factor(jnp.cos(theta))
    col_re, col_im = factor(jnp.sin(theta))
    table = table_ref[pl.ds(pl.multiple_of(block_map[ids[0]] * rows, rows), rows), :]
    for k in range(blocks):
        at = slice(k * rows, (k + 1) * rows)
        left[at, :pupil] = (table * row_re[k : k + 1]).astype(left.dtype)
        left[at, pupil:] = (table * row_im[k : k + 1]).astype(left.dtype)

    def first(j):
        real = base[:, :pupil]
        imag = base[:, pupil:]
        if j >= 0:
            value = modes_ref[:, j * height : (j + 1) * height].reshape(pupil, pupil)
            real, imag = -value * imag, value * real
        slot = right.at[j % 2]
        slot[:pupil, :pupil] = real
        slot[:pupil, pupil:] = imag
        slot[pupil:, :pupil] = -imag
        slot[pupil:, pupil:] = real
        return jnp.dot(left[...], slot[...], preferred_element_type=jnp.float32)

    def second(t):
        parts = ([], [])
        for k in range(blocks):
            t_re, t_im = t[k * rows : (k + 1) * rows, :pupil], t[k * rows : (k + 1) * rows, pupil:]
            c_re, c_im = col_re[k : k + 1], col_im[k : k + 1]
            parts[0].append(t_re * c_re - t_im * c_im)
            parts[1].append(t_re * c_im + t_im * c_re)
        mixed = jnp.concatenate(parts[0] + parts[1], axis=0).astype(jnp.bfloat16)
        return jnp.dot(mixed, second_ref[...], preferred_element_type=jnp.float32)

    def third(j, d):
        if j < 0:
            own[...] = d * (2.0 * 4.0 / blocks)
            return
        total = jnp.zeros((rows, length), jnp.float32)
        for k in range(2 * blocks):
            at = slice(k * rows, (k + 1) * rows)
            total += own[at] * d[at]
        out_ref[:, j, :] = total

    firsts, seconds = {}, {}
    for step in range(count + 3):
        if step <= count:
            firsts[step] = first(step - 1)
        if 0 <= step - 1 <= count:
            seconds[step - 1] = second(firsts.pop(step - 1))
        if 0 <= step - 2 <= count:
            third(step - 3, seconds.pop(step - 2))


def local(mod_points, pupil_mask, phase_offset, modes, block_map):
    count, height, pupil = modes.shape
    blocks = lax.axis_size("mod")
    group = lax.axis_size("mode")
    length = 2 * pupil
    rows = length // blocks
    mark = jnp.broadcast_to(mod_points.astype(jnp.bfloat16)[:, None], (8, pupil))
    packed = jnp.concatenate([modes.reshape(count * height, pupil), mark])
    spread = jnp.broadcast_to(packed[None], (blocks,) + packed.shape)
    gathered = lax.all_to_all(spread, "mod", 0, 0)

    mask = pupil_mask.astype(jnp.float32)
    field = jnp.concatenate([mask * jnp.cos(phase_offset), mask * jnp.sin(phase_offset)]).astype(jnp.bfloat16)
    pairs = lambda t0, t1: [(i, i ^ (2 * (t1 if i & 1 else t0))) for i in range(group)]
    cores = [(i, i ^ 1) for i in range(group)]
    pair = jnp.stack([field, lax.ppermute(field, "mode", cores)])
    near = jnp.stack([lax.ppermute(pair, "mode", pairs(t, t + 4)) for t in range(1, 4)])
    fourth = lax.ppermute(pair, "mode", pairs(4, 4))
    far = lax.ppermute(near, "mode", cores)

    table = sensor_table(length, pupil)
    ids = jnp.stack([lax.axis_index("mod"), lax.axis_index("mode")]).astype(jnp.int32)
    vmem = pl.BlockSpec(memory_space=pltpu.VMEM)
    smem = pl.BlockSpec(memory_space=pltpu.SMEM)
    return pl.pallas_call(
        tangent_kernel,
        in_specs=[smem, smem] + [vmem] * 7,
        out_specs=vmem,
        out_shape=jax.ShapeDtypeStruct((rows, count, length), jnp.float32),
        scratch_shapes=[
            pltpu.VMEM((length, length), jnp.bfloat16),
            pltpu.VMEM((pupil, length), jnp.bfloat16),
            pltpu.VMEM((2, length, length), jnp.bfloat16),
            pltpu.VMEM((2 * length, length), jnp.float32),
        ],
        compiler_params=pltpu.CompilerParams(vmem_limit_bytes=24 * 2**20),
        cost_estimate=pl.CostEstimate(flops=2_700_000_000, bytes_accessed=2_000_000, transcendentals=0),
        name="tangent",
    )(
        block_map,
        ids,
        gathered,
        pair,
        near,
        fourth,
        far,
        jnp.asarray(table, jnp.float32),
        jnp.asarray(table.T, jnp.bfloat16),
    )


def solution(mesh):
    placed = (P("mod"), P("mode", None), P("mode", None), P("mode", "mod", None), P())
    return jax.shard_map(
        local, mesh=mesh, in_specs=placed, out_specs=P("mod", "mode", None), check_vma=False
    )
```

```python
import math

import jax
import jax.numpy as jnp
import numpy as np
from jax import lax
from jax.experimental import pallas as pl
from jax.experimental.pallas import tpu as pltpu
from jax.sharding import PartitionSpec as P

NPTS = 48
radius_cells = 6.0


def peer_order(blocks):
    chips = blocks // 2
    return [2 * (chips - 1 - i % chips) + i // chips for i in range(blocks)]


def sensor_table(length, pupil):
    c = np.arange(length) - length // 2
    n = np.arange(pupil) - pupil // 2
    s = c[:, None] + n[None, :]
    odd = s % 2 != 0
    with np.errstate(divide="ignore"):
        kernel = 2.0 / (length * np.cos(2.0 * np.pi * s / length))
    shift = np.abs(s % length - length // 2) == length // 4
    direct = np.where(shift, np.where(n % 2 == 0, 0.5, -0.5)[None, :], 0.0)
    return np.where(odd, kernel, direct)


def tangent_kernel(block_map, ids, modes_ref, pair_ref, near_ref, fourth_ref, far_ref, table_ref, second_ref, out_ref, left, base, right, own):
    blocks = modes_ref.shape[0]
    length, pupil = table_ref.shape
    rows = length // blocks
    height = pupil // blocks
    count = out_ref.shape[1]
    half_group = blocks // 2
    me = ids[1]
    core = me & 1
    found = []
    for r in range(2):
        found.append((pair_ref[r], me ^ r))
        found.append((fourth_ref[r], me ^ (8 + r)))
        for i in range(3):
            found.append((near_ref[i, r], me ^ (2 * (i + 1 + 4 * core) + r)))
            found.append((far_ref[i, r], me ^ (2 * (i + 5 - 4 * core) + 1 - r)))
    for part, block in found:
        at = pl.multiple_of(((block & 1) * half_group + half_group - 1 - (block >> 1)) * height, height)
        base[pl.ds(at, height), :pupil] = part[:height]
        base[pl.ds(at, height), pupil:] = part[height:]
    point = jnp.concatenate([modes_ref[i][count * height :].astype(jnp.float32)[:1] for i in range(blocks)], axis=0)
    theta = point * (2.0 * math.pi / NPTS)
    scale = 2.0 * math.pi * radius_cells / length
    place = lax.broadcasted_iota(jnp.int32, (blocks, pupil), 1)
    odd = (place & 1) == 1
    block = place // height
    row = (2 * (half_group - 1 - block % half_group) + block // half_group) * height + place % height

    def factor(tilt, index):
        angle = tilt * ((index - pupil // 2).astype(jnp.float32) * scale)
        cos, sin = jnp.cos(angle), jnp.sin(angle)
        return jnp.where(odd, -sin, cos), jnp.where(odd, cos, sin)

    row_re, row_im = factor(jnp.cos(theta), row)
    col_re, col_im = factor(jnp.sin(theta), place)
    table = table_ref[pl.ds(pl.multiple_of(block_map[ids[0]] * rows, rows), rows), :]
    for k in range(blocks):
        at = slice(k * rows, (k + 1) * rows)
        left[at, :pupil] = (table * row_re[k : k + 1]).astype(left.dtype)
        left[at, pupil:] = (table * row_im[k : k + 1]).astype(left.dtype)

    def first(j):
        real = base[:, :pupil]
        imag = base[:, pupil:]
        if j >= 0:
            value = modes_ref[:, j * height : (j + 1) * height].reshape(pupil, pupil)
            real, imag = -value * imag, value * real
        slot = right.at[j % 2]
        slot[:pupil, :pupil] = real
        slot[:pupil, pupil:] = imag
        slot[pupil:, :pupil] = -imag
        slot[pupil:, pupil:] = real
        return jnp.dot(left[...], slot[...], preferred_element_type=jnp.float32)

    def second(t):
        parts = ([], [])
        for k in range(blocks):
            t_re, t_im = t[k * rows : (k + 1) * rows, :pupil], t[k * rows : (k + 1) * rows, pupil:]
            c_re, c_im = col_re[k : k + 1], col_im[k : k + 1]
            parts[0].append(t_re * c_re - t_im * c_im)
            parts[1].append(t_re * c_im + t_im * c_re)
        mixed = jnp.concatenate(parts[0] + parts[1], axis=0).astype(jnp.bfloat16)
        return jnp.dot(mixed, second_ref[...], preferred_element_type=jnp.float32)

    def third(j, d):
        if j < 0:
            own[...] = d * (2.0 * 4.0 / blocks)
            return
        total = jnp.zeros((rows, length), jnp.float32)
        for k in range(2 * blocks):
            at = slice(k * rows, (k + 1) * rows)
            total += own[at] * d[at]
        out_ref[:, j, :] = total

    firsts, seconds = {}, {}
    for step in range(count + 3):
        if step <= count:
            firsts[step] = first(step - 1)
        if 0 <= step - 1 <= count:
            seconds[step - 1] = second(firsts.pop(step - 1))
        if 0 <= step - 2 <= count:
            third(step - 3, seconds.pop(step - 2))


def local(mod_points, pupil_mask, phase_offset, modes, block_map):
    count, height, pupil = modes.shape
    blocks = lax.axis_size("mod")
    group = lax.axis_size("mode")
    length = 2 * pupil
    rows = length // blocks
    order = peer_order(blocks)
    mark = jnp.broadcast_to(mod_points.astype(jnp.bfloat16)[:, None], (8, pupil))
    packed = jnp.concatenate([modes.reshape(count * height, pupil), mark])
    spread = jnp.broadcast_to(packed[None], (blocks,) + packed.shape)
    gathered = lax.all_to_all(spread, "mod", 0, 0, axis_index_groups=[order])

    mask = pupil_mask.astype(jnp.float32)
    field = jnp.concatenate([mask * jnp.cos(phase_offset), mask * jnp.sin(phase_offset)]).astype(jnp.bfloat16)
    pairs = lambda t0, t1: [(i, i ^ (2 * (t1 if i & 1 else t0))) for i in range(group)]
    cores = [(i, i ^ 1) for i in range(group)]
    pair = jnp.stack([field, lax.ppermute(field, "mode", cores)])
    near = jnp.stack([lax.ppermute(pair, "mode", pairs(t, t + 4)) for t in range(1, 4)])
    fourth = lax.ppermute(pair, "mode", pairs(4, 4))
    far = lax.ppermute(near, "mode", cores)

    table = sensor_table(length, pupil)
    places = np.concatenate([np.arange(height) + b * height for b in order])
    ids = jnp.stack([lax.axis_index("mod"), lax.axis_index("mode")]).astype(jnp.int32)
    vmem = pl.BlockSpec(memory_space=pltpu.VMEM)
    smem = pl.BlockSpec(memory_space=pltpu.SMEM)
    return pl.pallas_call(
        tangent_kernel,
        in_specs=[smem, smem] + [vmem] * 7,
        out_specs=vmem,
        out_shape=jax.ShapeDtypeStruct((rows, count, length), jnp.float32),
        scratch_shapes=[
            pltpu.VMEM((length, length), jnp.bfloat16),
            pltpu.VMEM((pupil, length), jnp.bfloat16),
            pltpu.VMEM((2, length, length), jnp.bfloat16),
            pltpu.VMEM((2 * length, length), jnp.float32),
        ],
        compiler_params=pltpu.CompilerParams(vmem_limit_bytes=24 * 2**20),
        cost_estimate=pl.CostEstimate(flops=2_700_000_000, bytes_accessed=2_000_000, transcendentals=0),
        name="tangent",
    )(
        block_map,
        ids,
        gathered,
        pair,
        near,
        fourth,
        far,
        jnp.asarray(table[:, places], jnp.float32),
        jnp.asarray(table.T, jnp.bfloat16),
    )


def solution(mesh):
    placed = (P("mod"), P("mode", None), P("mode", None), P("mode", "mod", None), P())
    return jax.shard_map(
        local, mesh=mesh, in_specs=placed, out_specs=P("mod", "mode", None), check_vma=False
    )
```

```python
import math

import jax
import jax.numpy as jnp
import numpy as np
from jax import lax
from jax.experimental import pallas as pl
from jax.experimental.pallas import tpu as pltpu
from jax.sharding import PartitionSpec as P

NPTS = 48
radius_cells = 6.0


def peer_order(blocks):
    chips = blocks // 2
    return [2 * (chips - 1 - i % chips) + i // chips for i in range(blocks)]


def sensor_table(length, pupil):
    c = np.arange(length) - length // 2
    n = np.arange(pupil) - pupil // 2
    s = c[:, None] + n[None, :]
    odd = s % 2 != 0
    with np.errstate(divide="ignore"):
        kernel = 2.0 / (length * np.cos(2.0 * np.pi * s / length))
    shift = np.abs(s % length - length // 2) == length // 4
    direct = np.where(shift, np.where(n % 2 == 0, 0.5, -0.5)[None, :], 0.0)
    return np.where(odd, kernel, direct)


def tangent_kernel(block_map, ids, modes_ref, pair_ref, near_ref, fourth_ref, far_ref, table_ref, second_ref, out_ref, left, base, right, own):
    blocks = modes_ref.shape[0]
    length, pupil = table_ref.shape
    rows = length // blocks
    height = pupil // blocks
    count = out_ref.shape[1]
    half_group = blocks // 2
    me = ids[1]
    core = me & 1
    found = []
    for r in range(2):
        found.append((pair_ref[r], me ^ r))
        found.append((fourth_ref[r], me ^ (8 + r)))
        for i in range(3):
            found.append((near_ref[i, r], me ^ (2 * (i + 5 - 4 * core) + r)))
            found.append((far_ref[i, r], me ^ (2 * (i + 1 + 4 * core) + 1 - r)))
    for part, block in found:
        at = pl.multiple_of(((block & 1) * half_group + half_group - 1 - (block >> 1)) * height, height)
        base[pl.ds(at, height), :pupil] = part[:height]
        base[pl.ds(at, height), pupil:] = part[height:]
    point = jnp.concatenate([modes_ref[i][count * height :].astype(jnp.float32)[:1] for i in range(blocks)], axis=0)
    theta = point * (2.0 * math.pi / NPTS)
    scale = 2.0 * math.pi * radius_cells / length
    place = lax.broadcasted_iota(jnp.int32, (blocks, pupil), 1)
    odd = (place & 1) == 1
    block = place // height
    row = (2 * (half_group - 1 - block % half_group) + block // half_group) * height + place % height

    def factor(tilt, index):
        angle = tilt * ((index - pupil // 2).astype(jnp.float32) * scale)
        cos, sin = jnp.cos(angle), jnp.sin(angle)
        return jnp.where(odd, -sin, cos), jnp.where(odd, cos, sin)

    row_re, row_im = factor(jnp.cos(theta), row)
    col_re, col_im = factor(jnp.sin(theta), place)
    table = table_ref[pl.ds(pl.multiple_of(block_map[ids[0]] * rows, rows), rows), :]
    for k in range(blocks):
        at = slice(k * rows, (k + 1) * rows)
        left[at, :pupil] = (table * row_re[k : k + 1]).astype(left.dtype)
        left[at, pupil:] = (table * row_im[k : k + 1]).astype(left.dtype)

    def first(j):
        real = base[:, :pupil]
        imag = base[:, pupil:]
        if j >= 0:
            value = modes_ref[:, j * height : (j + 1) * height].reshape(pupil, pupil)
            real, imag = -value * imag, value * real
        slot = right.at[j % 2]
        slot[:pupil, :pupil] = real
        slot[:pupil, pupil:] = imag
        slot[pupil:, :pupil] = -imag
        slot[pupil:, pupil:] = real
        return jnp.dot(left[...], slot[...], preferred_element_type=jnp.float32)

    def second(t):
        parts = ([], [])
        for k in range(blocks):
            t_re, t_im = t[k * rows : (k + 1) * rows, :pupil], t[k * rows : (k + 1) * rows, pupil:]
            c_re, c_im = col_re[k : k + 1], col_im[k : k + 1]
            parts[0].append(t_re * c_re - t_im * c_im)
            parts[1].append(t_re * c_im + t_im * c_re)
        mixed = jnp.concatenate(parts[0] + parts[1], axis=0).astype(jnp.bfloat16)
        return jnp.dot(mixed, second_ref[...], preferred_element_type=jnp.float32)

    def third(j, d):
        if j < 0:
            own[...] = d * (2.0 * 4.0 / blocks)
            return
        total = jnp.zeros((rows, length), jnp.float32)
        for k in range(2 * blocks):
            at = slice(k * rows, (k + 1) * rows)
            total += own[at] * d[at]
        out_ref[:, j, :] = total

    firsts, seconds = {}, {}
    for step in range(count + 3):
        if step <= count:
            firsts[step] = first(step - 1)
        if 0 <= step - 1 <= count:
            seconds[step - 1] = second(firsts.pop(step - 1))
        if 0 <= step - 2 <= count:
            third(step - 3, seconds.pop(step - 2))


def local(mod_points, pupil_mask, phase_offset, modes, block_map):
    count, height, pupil = modes.shape
    blocks = lax.axis_size("mod")
    group = lax.axis_size("mode")
    length = 2 * pupil
    rows = length // blocks
    order = peer_order(blocks)
    mark = jnp.broadcast_to(mod_points.astype(jnp.bfloat16)[:, None], (8, pupil))
    packed = jnp.concatenate([modes.reshape(count * height, pupil), mark])
    spread = jnp.broadcast_to(packed[None], (blocks,) + packed.shape)
    gathered = lax.all_to_all(spread, "mod", 0, 0, axis_index_groups=[order])

    mask = pupil_mask.astype(jnp.float32)
    field = jnp.concatenate([mask * jnp.cos(phase_offset), mask * jnp.sin(phase_offset)]).astype(jnp.bfloat16)
    pairs = lambda t0, t1: [(i, i ^ (2 * (t1 if i & 1 else t0))) for i in range(group)]
    cores = [(i, i ^ 1) for i in range(group)]
    pair = jnp.stack([field, lax.ppermute(field, "mode", cores)])
    near = jnp.stack([lax.ppermute(pair, "mode", pairs(t + 4, t)) for t in range(1, 4)])
    fourth = lax.ppermute(pair, "mode", pairs(4, 4))
    far = lax.ppermute(near, "mode", cores)

    table = sensor_table(length, pupil)
    places = np.concatenate([np.arange(height) + b * height for b in order])
    ids = jnp.stack([lax.axis_index("mod"), lax.axis_index("mode")]).astype(jnp.int32)
    vmem = pl.BlockSpec(memory_space=pltpu.VMEM)
    smem = pl.BlockSpec(memory_space=pltpu.SMEM)
    return pl.pallas_call(
        tangent_kernel,
        in_specs=[smem, smem] + [vmem] * 7,
        out_specs=vmem,
        out_shape=jax.ShapeDtypeStruct((rows, count, length), jnp.float32),
        scratch_shapes=[
            pltpu.VMEM((length, length), jnp.bfloat16),
            pltpu.VMEM((pupil, length), jnp.bfloat16),
            pltpu.VMEM((2, length, length), jnp.bfloat16),
            pltpu.VMEM((2 * length, length), jnp.float32),
        ],
        compiler_params=pltpu.CompilerParams(vmem_limit_bytes=24 * 2**20),
        cost_estimate=pl.CostEstimate(flops=2_700_000_000, bytes_accessed=2_000_000, transcendentals=0),
        name="tangent",
    )(
        block_map,
        ids,
        gathered,
        pair,
        near,
        fourth,
        far,
        jnp.asarray(table[:, places], jnp.float32),
        jnp.asarray(table.T, jnp.bfloat16),
    )


def solution(mesh):
    placed = (P("mod"), P("mode", None), P("mode", None), P("mode", "mod", None), P())
    return jax.shard_map(
        local, mesh=mesh, in_specs=placed, out_specs=P("mod", "mode", None), check_vma=False
    )
```

```python
import math

import jax
import jax.numpy as jnp
import numpy as np
from jax import lax
from jax.experimental import pallas as pl
from jax.experimental.pallas import tpu as pltpu
from jax.sharding import PartitionSpec as P

NPTS = 48
radius_cells = 6.0


def peer_order(blocks):
    chips = blocks // 2
    return [2 * (3 * i % chips) + i // chips for i in range(blocks)]


def sensor_table(length, pupil):
    c = np.arange(length) - length // 2
    n = np.arange(pupil) - pupil // 2
    s = c[:, None] + n[None, :]
    odd = s % 2 != 0
    with np.errstate(divide="ignore"):
        kernel = 2.0 / (length * np.cos(2.0 * np.pi * s / length))
    shift = np.abs(s % length - length // 2) == length // 4
    direct = np.where(shift, np.where(n % 2 == 0, 0.5, -0.5)[None, :], 0.0)
    return np.where(odd, kernel, direct)


def tangent_kernel(block_map, ids, modes_ref, pair_ref, near_ref, fourth_ref, far_ref, table_ref, second_ref, out_ref, left, base, right, own):
    blocks = modes_ref.shape[0]
    length, pupil = table_ref.shape
    rows = length // blocks
    height = pupil // blocks
    count = out_ref.shape[1]
    half_group = blocks // 2
    me = ids[1]
    core = me & 1
    found = []
    for r in range(2):
        found.append((pair_ref[r], me ^ r))
        found.append((fourth_ref[r], me ^ (8 + r)))
        for i in range(3):
            found.append((near_ref[i, r], me ^ (2 * (i + 5 - 4 * core) + r)))
            found.append((far_ref[i, r], me ^ (2 * (i + 1 + 4 * core) + 1 - r)))
    for part, block in found:
        at = pl.multiple_of(((block & 1) * half_group + ((3 * (block >> 1)) & (half_group - 1))) * height, height)
        base[pl.ds(at, height), :pupil] = part[:height]
        base[pl.ds(at, height), pupil:] = part[height:]
    point = jnp.concatenate([modes_ref[i][count * height :].astype(jnp.float32)[:1] for i in range(blocks)], axis=0)
    theta = point * (2.0 * math.pi / NPTS)
    scale = 2.0 * math.pi * radius_cells / length
    place = lax.broadcasted_iota(jnp.int32, (blocks, pupil), 1)
    odd = (place & 1) == 1
    block = place // height
    row = (2 * (3 * block % half_group) + block // half_group) * height + place % height

    def factor(tilt, index):
        angle = tilt * ((index - pupil // 2).astype(jnp.float32) * scale)
        cos, sin = jnp.cos(angle), jnp.sin(angle)
        return jnp.where(odd, -sin, cos), jnp.where(odd, cos, sin)

    row_re, row_im = factor(jnp.cos(theta), row)
    col_re, col_im = factor(jnp.sin(theta), place)
    table = table_ref[pl.ds(pl.multiple_of(block_map[ids[0]] * rows, rows), rows), :]
    for k in range(blocks):
        at = slice(k * rows, (k + 1) * rows)
        left[at, :pupil] = (table * row_re[k : k + 1]).astype(left.dtype)
        left[at, pupil:] = (table * row_im[k : k + 1]).astype(left.dtype)

    def first(j):
        real = base[:, :pupil]
        imag = base[:, pupil:]
        if j >= 0:
            value = modes_ref[:, j * height : (j + 1) * height].reshape(pupil, pupil)
            real, imag = -value * imag, value * real
        slot = right.at[j % 2]
        slot[:pupil, :pupil] = real
        slot[:pupil, pupil:] = imag
        slot[pupil:, :pupil] = -imag
        slot[pupil:, pupil:] = real
        return jnp.dot(left[...], slot[...], preferred_element_type=jnp.float32)

    def second(t):
        parts = ([], [])
        for k in range(blocks):
            t_re, t_im = t[k * rows : (k + 1) * rows, :pupil], t[k * rows : (k + 1) * rows, pupil:]
            c_re, c_im = col_re[k : k + 1], col_im[k : k + 1]
            parts[0].append(t_re * c_re - t_im * c_im)
            parts[1].append(t_re * c_im + t_im * c_re)
        mixed = jnp.concatenate(parts[0] + parts[1], axis=0).astype(jnp.bfloat16)
        return jnp.dot(mixed, second_ref[...], preferred_element_type=jnp.float32)

    def third(j, d):
        if j < 0:
            own[...] = d * (2.0 * 4.0 / blocks)
            return
        total = jnp.zeros((rows, length), jnp.float32)
        for k in range(2 * blocks):
            at = slice(k * rows, (k + 1) * rows)
            total += own[at] * d[at]
        out_ref[:, j, :] = total

    firsts, seconds = {}, {}
    for step in range(count + 3):
        if step <= count:
            firsts[step] = first(step - 1)
        if 0 <= step - 1 <= count:
            seconds[step - 1] = second(firsts.pop(step - 1))
        if 0 <= step - 2 <= count:
            third(step - 3, seconds.pop(step - 2))


def local(mod_points, pupil_mask, phase_offset, modes, block_map):
    count, height, pupil = modes.shape
    blocks = lax.axis_size("mod")
    group = lax.axis_size("mode")
    length = 2 * pupil
    rows = length // blocks
    order = peer_order(blocks)
    mark = jnp.broadcast_to(mod_points.astype(jnp.bfloat16)[:, None], (8, pupil))
    packed = jnp.concatenate([modes.reshape(count * height, pupil), mark])
    spread = jnp.broadcast_to(packed[None], (blocks,) + packed.shape)
    gathered = lax.all_to_all(spread, "mod", 0, 0, axis_index_groups=[order])

    mask = pupil_mask.astype(jnp.float32)
    field = jnp.concatenate([mask * jnp.cos(phase_offset), mask * jnp.sin(phase_offset)]).astype(jnp.bfloat16)
    pairs = lambda t0, t1: [(i, i ^ (2 * (t1 if i & 1 else t0))) for i in range(group)]
    cores = [(i, i ^ 1) for i in range(group)]
    pair = jnp.stack([field, lax.ppermute(field, "mode", cores)])
    near = jnp.stack([lax.ppermute(pair, "mode", pairs(t + 4, t)) for t in range(1, 4)])
    fourth = lax.ppermute(pair, "mode", pairs(4, 4))
    far = lax.ppermute(near, "mode", cores)

    table = sensor_table(length, pupil)
    places = np.concatenate([np.arange(height) + b * height for b in order])
    ids = jnp.stack([lax.axis_index("mod"), lax.axis_index("mode")]).astype(jnp.int32)
    vmem = pl.BlockSpec(memory_space=pltpu.VMEM)
    smem = pl.BlockSpec(memory_space=pltpu.SMEM)
    return pl.pallas_call(
        tangent_kernel,
        in_specs=[smem, smem] + [vmem] * 7,
        out_specs=vmem,
        out_shape=jax.ShapeDtypeStruct((rows, count, length), jnp.float32),
        scratch_shapes=[
            pltpu.VMEM((length, length), jnp.bfloat16),
            pltpu.VMEM((pupil, length), jnp.bfloat16),
            pltpu.VMEM((2, length, length), jnp.bfloat16),
            pltpu.VMEM((2 * length, length), jnp.float32),
        ],
        compiler_params=pltpu.CompilerParams(vmem_limit_bytes=24 * 2**20),
        cost_estimate=pl.CostEstimate(flops=2_700_000_000, bytes_accessed=2_000_000, transcendentals=0),
        name="tangent",
    )(
        block_map,
        ids,
        gathered,
        pair,
        near,
        fourth,
        far,
        jnp.asarray(table[:, places], jnp.float32),
        jnp.asarray(table.T, jnp.bfloat16),
    )


def solution(mesh):
    placed = (P("mod"), P("mode", None), P("mode", None), P("mode", "mod", None), P())
    return jax.shard_map(
        local, mesh=mesh, in_specs=placed, out_specs=P("mod", "mode", None), check_vma=False
    )
```
